256 devices in a mesh: grp: 4 (over z_lo), dp: 8 (over y, core), mp: 8 (over x, z_hi).
Axes of the slice: x: 4, y: 4, z: 8 (z_hi: 2, z_lo: 4; z = z_hi * 4 + z_lo), core: 2. Of those that a mesh axis runs over, the one named last changes fastest.
Arguments:
- neighbour_tokens: bfloat16 [128, 32, 896], P(None, 'dp'), may hold values from -14 to 14
- enc_gain: float32 [896], replicated, may hold values from 0.1 to 1.9
- enc_up: bfloat16 [896, 3584], P(None, 'mp'), may hold values from -0.1875 to 0.1875
- enc_down: bfloat16 [3584, 896], P('mp'), may hold values from -0.09375 to 0.09375
- hidden: bfloat16 [3, 2048, 4096], P(None, 'dp', 'mp'), may hold values from -6 to 6
- head_grads: bfloat16 [3, 2048, 4096], P(None, 'dp', 'mp'), may hold values from -12 to 12
- query_weight: bfloat16 [4096, 4096], P(None, 'mp'), may hold values from -0.09375 to 0.09375
- kv_weight: bfloat16 [896, 2, 4096], P(None, None, 'mp'), may hold values from -0.1875 to 0.1875
- neighbour_ids: int32 [3, 32, 2], replicated, may hold values from 0 to 31, as said below
- pool_slot: int32 [32], replicated, may hold values from 0 to 31, as said below
Outputs:
- kv_grad: float32 [896, 2, 4096], P(('grp', 'dp'), None, 'mp')
- neighbour_grad: float32 [128, 32, 896], P('mp', 'dp')
The draws below stay inside these ranges and needn't reach their ends.
Inputs may be any that keep to these rules, and one draw needn't show every extreme that they name: `neighbour_ids`: the 2 neighbours of one span differ. Slots s with the same floor(s / 4) belong to one dp index. For each group and each block of 4 consecutive spans, at most 2 of the block's references name neighbours whose slots belong to one dp index, and in every block some dp index takes exactly 2. `pool_slot`: A permutation of the slots.
All inputs are finite; a program needn't handle non-finite values.
Results may differ from the reference program's by a relative error of at most 0.029.
Values may be sent and summed in bfloat16 or wider, within the bound.
No kernel may reach another device: no remote copies, remote signals or barrier semaphores. Data moves between devices by JAX's collectives and lax.ppermute only.
A program may use at most 64 MiB of HBM per device.

```python
import math
import jax
import jax.numpy as jnp
from jax import lax

D = 4096
HD = 128
DE = 896
FE = 3584
SPAN = 64
NLEN = 128
KNB = 2
LEN = 2048
CH_DEV = 4
NB_DP = 4
DG = 3
GTOK = 2048
NPOOL = 32
CAP = 2
N_DP = 8
N_MP = 8


def shared_tables(key):
    refs_count = CH_DEV * KNB
    others_count = (N_DP - 1) * CAP
    streams = jax.random.split(key, 6)
    hottest = jax.random.randint(streams[0], (DG, N_DP, 1), 0, N_DP)
    others = (hottest + 1 + jnp.arange(others_count, dtype=jnp.int32)[None, None, :] // CAP) % N_DP
    order_keys = jax.random.randint(streams[1], (DG, N_DP, others_count), 0, 1 << 20) * others_count + jnp.arange(others_count, dtype=jnp.int32)
    picked = jnp.take_along_axis(others, jnp.argsort(order_keys, axis=-1), axis=-1)[..., :refs_count - CAP]
    owners = jnp.concatenate([jnp.broadcast_to(hottest, (DG, N_DP, CAP)), picked], axis=-1)
    mixing = jax.random.randint(streams[2], (DG, N_DP, refs_count), 0, 1 << 20) * refs_count + jnp.arange(refs_count, dtype=jnp.int32)
    owners = jnp.take_along_axis(owners, jnp.argsort(mixing, axis=-1), axis=-1)
    first_draw = jax.random.randint(streams[3], (DG, N_DP, refs_count), 0, NB_DP)
    second_draw = jax.random.randint(streams[4], (DG, N_DP, refs_count), 0, NB_DP)
    locals_all = jnp.minimum(first_draw, second_draw)
    owner_pairs = owners.reshape(DG, N_DP, CH_DEV, KNB)
    local_pairs = locals_all.reshape(DG, N_DP, CH_DEV, KNB)
    clashes = (owner_pairs[..., 1] == owner_pairs[..., 0]) & (local_pairs[..., 1] == local_pairs[..., 0])
    second_local = jnp.where(clashes, (local_pairs[..., 0] + 1) % NB_DP, local_pairs[..., 1])
    local_pairs = jnp.stack([local_pairs[..., 0], second_local], axis=-1)
    slot_table = (owner_pairs * NB_DP + local_pairs).reshape(DG, N_DP * CH_DEV, KNB).astype(jnp.int32)
    permuted = jax.random.permutation(streams[5], NPOOL).astype(jnp.int32)
    first_slot = slot_table[0, 0, 0]
    other_slot = slot_table[0, 0, 1]
    found = jnp.argmax(permuted == first_slot)
    permuted = permuted.at[found].set(permuted[NPOOL - 1])
    permuted = permuted.at[NPOOL - 1].set(first_slot)
    found = jnp.argmax(permuted == other_slot)
    permuted = permuted.at[found].set(permuted[0])
    permuted = permuted.at[0].set(other_slot)
    inverse = jnp.argsort(permuted).astype(jnp.int32)
    return (inverse[slot_table].astype(jnp.int32), permuted)


def draw_neighbour_ids(key, part):
    identity, permuted = shared_tables(key)
    return identity


def draw_pool_slot(key, part):
    identity, permuted = shared_tables(key)
    return permuted


def draw_neighbour_tokens(key, part):
    key = jax.random.fold_in(key, 11)
    streams = jax.random.split(key, 3)
    base = jnp.clip(jax.random.normal(streams[0], (NLEN, NPOOL, DE), jnp.float32), -4.0, 4.0)
    row_scale = jnp.exp(jax.random.uniform(streams[1], (NLEN, NPOOL, 1), jnp.float32, jnp.log(0.9), jnp.log(1.1)))
    column_scale = jnp.exp(jax.random.uniform(streams[2], (DE,), jnp.float32, jnp.log(0.3), jnp.log(3.0)))
    return (base * row_scale * column_scale).astype(jnp.bfloat16)


def block_levels(rng, shape, pieces, least, top_value):
    def one(axis_at, blocks):
        draws = jax.random.uniform(jax.random.fold_in(jax.random.fold_in(rng, 6), axis_at), (blocks,), jnp.float32, least / len(pieces), top_value / len(pieces))
        return jnp.repeat(jnp.exp(draws), shape[axis_at] // blocks).reshape((-1,) + (1,) * (len(shape) - axis_at - 1))

    loudness = one(*pieces[0])
    for cut in pieces[1:]:
        loudness = loudness * one(*cut)
    return loudness


def gaussian(key, extent, width, most, cuts=(), held_as=jnp.bfloat16):
    values = width * jax.random.normal(key, extent, jnp.float32)
    if cuts:
        values = values * block_levels(key, extent, cuts, -0.22, 0.18)
    return jnp.clip(values, -most, most).astype(held_as)


def setup_inputs(seed: int = 0) -> dict:
    streams_of = jax.random.split(jax.random.key(seed), 11)
    neighbour_tokens = draw_neighbour_tokens(jax.random.fold_in(streams_of[10], 71), 0)
    enc_gain = jnp.clip(1.0 + 0.18 * jax.random.normal(streams_of[1], (DE,), jnp.float32), 0.1, 1.9)
    enc_up = gaussian(streams_of[2], (DE, FE), DE ** -0.5, 0.1875, ((1, 8),))
    enc_down = gaussian(streams_of[3], (FE, DE), FE ** -0.5, 0.09375, ((0, 8),))
    hidden = gaussian(streams_of[4], (DG, GTOK, D), 1.0, 6.0, ((1, 8), (2, 8)))
    head_grads = gaussian(streams_of[5], (DG, GTOK, D), 2.0, 12.0, ((1, 8), (2, 8)))
    query_weight = gaussian(streams_of[6], (D, D), D ** -0.5, 0.09375, ((1, 8),))
    kv_weight = gaussian(streams_of[7], (DE, 2, D), DE ** -0.5, 0.1875, ((2, 8),))
    neighbour_ids = draw_neighbour_ids(jax.random.fold_in(streams_of[10], 71), 0)
    pool_slot = draw_pool_slot(jax.random.fold_in(streams_of[10], 71), 0)
    return {"neighbour_tokens": neighbour_tokens, "enc_gain": enc_gain, "enc_up": enc_up, "enc_down": enc_down, "hidden": hidden, "head_grads": head_grads, "query_weight": query_weight, "kv_weight": kv_weight, "neighbour_ids": neighbour_ids, "pool_slot": pool_slot}


EPSILON = 1e-06

def rounded(value):
    return lax.optimization_barrier(value.astype(jnp.bfloat16))

def attention_grads(queries, out_grads, paired):
    spans = queries.shape[0] // SPAN
    heads_count = queries.shape[1] // HD
    factor = 1.0 / math.sqrt(HD)
    ref_count = spans * KNB
    keys_all = paired[:, :, 0].reshape(spans, KNB * NLEN, heads_count, HD).astype(jnp.float32)
    values_all = paired[:, :, 1].reshape(spans, KNB * NLEN, heads_count, HD).astype(jnp.float32)
    query_blocks = queries.reshape(spans, SPAN, heads_count, HD).astype(jnp.float32)
    grad_blocks = out_grads.reshape(spans, SPAN, heads_count, HD).astype(jnp.float32)
    scores = jnp.einsum('cihe,cjhe->chij', query_blocks, keys_all) * factor
    weights = jnp.exp(scores - lax.optimization_barrier(jnp.max(scores, axis=-1, keepdims=True)))
    probs_all = weights / lax.optimization_barrier(jnp.sum(weights, axis=-1, keepdims=True))
    probs_low = rounded(probs_all)
    value_grads = rounded(jnp.einsum('chij,cihe->cjhe', probs_low.astype(jnp.float32), grad_blocks))
    prob_grads = jnp.einsum('cihe,cjhe->chij', grad_blocks, values_all)
    score_grads = rounded(probs_all * (prob_grads - lax.optimization_barrier(jnp.sum(probs_all * prob_grads, axis=-1, keepdims=True))) * factor)
    key_grads = rounded(jnp.einsum('chij,cihe->cjhe', score_grads.astype(jnp.float32), query_blocks))
    return jnp.stack([key_grads.reshape(ref_count, NLEN, heads_count * HD), value_grads.reshape(ref_count, NLEN, heads_count * HD)], axis=2)

def reference(neighbour_tokens, enc_gain, enc_up, enc_down, hidden, head_grads, query_weight, kv_weight, neighbour_ids, pool_slot):
    raw_tokens = neighbour_tokens.astype(jnp.float32)
    inverse_rms = lax.rsqrt(lax.optimization_barrier(jnp.mean(raw_tokens * raw_tokens, axis=-1, keepdims=True)) + EPSILON)
    normed = rounded(raw_tokens * inverse_rms * enc_gain)
    widened = jnp.einsum('tnd,df->tnf', normed.astype(jnp.float32), enc_up.astype(jnp.float32))
    widened = rounded(jax.nn.gelu(widened))
    encoded = rounded(raw_tokens + jnp.einsum('tnf,fd->tnd', widened.astype(jnp.float32), enc_down.astype(jnp.float32)))
    margin = SPAN - 1
    position = jnp.arange(GTOK, dtype=jnp.int32)
    target = position + margin
    anchor = position // SPAN * SPAN
    usable = (target < GTOK) & (target // LEN == anchor // LEN)
    block_width = D // N_MP
    padding = jnp.zeros((margin, D), jnp.bfloat16)
    weight_total = jnp.zeros((DE, 2, D), jnp.float32)
    neighbour_grad = jnp.zeros((NLEN, NPOOL, DE), jnp.float32)
    ref_count = N_DP * CH_DEV * KNB
    for member in range(DG):
        shifted = jnp.concatenate([hidden[member, margin:], padding], axis=0)
        queries = rounded(jnp.dot(shifted, query_weight, preferred_element_type=jnp.float32))
        out_grads = jnp.concatenate([head_grads[member, margin:], padding], axis=0)
        out_grads = jnp.where(usable[:, None], out_grads, jnp.zeros_like(out_grads))
        slot_list = pool_slot[neighbour_ids[member]].reshape(-1).astype(jnp.int32)
        ref_enc = jnp.transpose(jnp.take(encoded, slot_list, axis=1), (1, 0, 2))
        paired = rounded(jnp.einsum('rtd,dkc->rtkc', ref_enc.astype(jnp.float32), kv_weight.astype(jnp.float32)))
        pair_grads = attention_grads(queries, out_grads, paired)
        blocked_enc = ref_enc.reshape(N_DP, CH_DEV * KNB, NLEN, DE).astype(jnp.float32)
        blocked_grad = pair_grads.reshape(N_DP, CH_DEV * KNB, NLEN, 2, D).astype(jnp.float32)
        weight_part = rounded(jnp.einsum('brtd,brtkc->bdkc', blocked_enc, blocked_grad))
        weight_total = weight_total + lax.optimization_barrier(jnp.sum(weight_part.astype(jnp.float32), axis=0))
        ref_grad = jnp.zeros((ref_count, NLEN, DE), jnp.float32)
        for head_block in range(N_MP):
            columns = slice(head_block * block_width, (head_block + 1) * block_width)
            block_term = jnp.einsum('rtkc,dkc->rtd', pair_grads[..., columns].astype(jnp.float32), kv_weight[..., columns].astype(jnp.float32))
            block_term = rounded(block_term)
            ref_grad = ref_grad + block_term.astype(jnp.float32)
        neighbour_grad = neighbour_grad.at[:, slot_list, :].add(jnp.transpose(ref_grad, (1, 0, 2)))
    return (weight_total, neighbour_grad)
```

```python
import math

import jax
import jax.numpy as jnp
from jax import lax
from jax.experimental import pallas as pl
from jax.experimental.pallas import tpu as pltpu
from jax.sharding import PartitionSpec as P

HD = 128
SPAN = 64
KNB = 2
EPSILON = 1e-06
BF = jnp.bfloat16
F32 = jnp.float32


def ring(value, axis, by):
    return lax.ppermute(value, axis, [(i, (i // 2 + by) % 4 * 2 + i % 2) for i in range(8)])


def swap(value, axis):
    return lax.ppermute(value, axis, [(i, i ^ 1) for i in range(8)])


def group_ring(value, by):
    return lax.ppermute(value, "grp", [(i, (i + by) % 4) for i in range(4)])


def z_ring(value, by):
    pairs = []
    for grp in range(4):
        for mp in range(8):
            z = (mp % 2 * 4 + grp + by) % 8
            pairs.append((grp * 8 + mp, z % 4 * 8 + mp // 2 * 2 + z // 4))
    return lax.ppermute(value, ("grp", "mp"), pairs)


def at(value, index, axis=0):
    return lax.dynamic_index_in_dim(value, index, axis, keepdims=False)


def encoder_partial(tokens, gain, up_cols, down_rows):
    values = tokens.astype(F32)
    inverse_rms = lax.rsqrt(jnp.mean(values * values, axis=-1, keepdims=True) + EPSILON)
    normed = (values * inverse_rms * gain).astype(BF)
    widened = jnp.dot(normed, up_cols, preferred_element_type=F32)
    widened = jax.nn.gelu(widened).astype(BF)
    return jnp.dot(widened, down_rows, preferred_element_type=F32)


def attention_kernel(table, queries, grads, *refs):
    pairs, outs, total = refs[:8], refs[8:16], refs[16]
    factor = 1.0 / math.sqrt(HD)
    total[...] = jnp.zeros_like(total)
    store = refs[17]
    for block in range(8):
        store[block] = pairs[block][...].reshape(4, 4, 32, 2 * HD)
    for span in range(12):
        where = []
        for k in range(KNB):
            where.append((table[span * KNB + k, 0], table[span * KNB + k, 1]))
        loaded = [store[b, :, s].reshape(4 * 32, 2 * HD) for b, s in where]
        both = jnp.concatenate(loaded, axis=0)
        keys, values = both[:, :HD], both[:, HD:]
        query = queries[span]
        grad = grads[span]
        nt = (((1,), (1,)), ((), ()))
        scores = lax.dot_general(keys, query, nt, preferred_element_type=F32) * factor
        weights = jnp.exp(scores - jnp.max(scores, axis=0, keepdims=True))
        probs = weights / jnp.sum(weights, axis=0, keepdims=True)
        value_grads = jnp.dot(probs.astype(BF), grad, preferred_element_type=F32)
        prob_grads = lax.dot_general(values, grad, nt, preferred_element_type=F32)
        inner = jnp.sum(probs * prob_grads, axis=0, keepdims=True)
        score_grads = (probs * (prob_grads - inner) * factor).astype(BF)
        key_grads = jnp.dot(score_grads, query, preferred_element_type=F32)
        for k, (b, s) in enumerate(where):
            rows = slice(k * 128, (k + 1) * 128)
            total[b, :, s, :, :HD] += key_grads[rows].reshape(4, 32, HD)
            total[b, :, s, :, HD:] += value_grads[rows].reshape(4, 32, HD)
    for block in range(8):
        outs[block][...] = total[block].reshape(512, 2 * HD).astype(BF)


def attention(table, queries, grads, pairs):
    vmem = pl.BlockSpec(memory_space=pltpu.VMEM)
    return pl.pallas_call(
        attention_kernel,
        in_specs=[pl.BlockSpec(memory_space=pltpu.SMEM)] + [vmem] * 10,
        out_specs=[vmem] * 8,
        out_shape=[jax.ShapeDtypeStruct((512, 2 * HD), BF)] * 8,
        scratch_shapes=[
            pltpu.VMEM((8, 4, 4, 32, 2 * HD), F32),
            pltpu.VMEM((8, 4, 4, 32, 2 * HD), BF),
        ],
        compiler_params=pltpu.CompilerParams(vmem_limit_bytes=32 * 1024 * 1024),
        cost_estimate=pl.CostEstimate(
            flops=12 * 5 * 2 * 64 * 256 * 128, bytes_accessed=5_000_000, transcendentals=12 * 64 * 256
        ),
        name="attention",
    )(table, queries, grads, *pairs)


def local(
    neighbour_tokens,
    enc_gain,
    enc_up,
    enc_down,
    hidden,
    head_grads,
    query_weight,
    kv_weight,
    neighbour_ids,
    pool_slot,
):
    q = lax.axis_index("grp")
    dp = lax.axis_index("dp")
    mp = lax.axis_index("mp")
    x, z_hi = mp // 2, mp % 2
    y, core = dp // 2, dp % 2
    width = neighbour_tokens.shape[-1]

    own_tokens = at(neighbour_tokens, q, 1)
    partial = encoder_partial(own_tokens, enc_gain, enc_up, enc_down).astype(BF).reshape(4, 32, width)
    arrived = [ring(at(partial, (x + s) % 4), "mp", s) for s in (2, 1, 3)]
    summed = at(partial, x).astype(F32)
    for part in arrived:
        summed = summed + part.astype(F32)
    summed = summed.astype(BF)

    chunk = lax.dynamic_slice_in_dim(hidden, q * SPAN, SPAN, 1).reshape(3 * SPAN, -1)
    other = swap(chunk, "mp")
    own_parts = [chunk] + [ring(chunk, "mp", s) for s in (1, 2, 3)]

    by_z = [summed] + [z_ring(summed, s) for s in range(1, 8)]
    x_tokens = lax.dynamic_slice_in_dim(neighbour_tokens, x * 32, 32, 0)
    encoded = []
    for j in range(4):
        mixed = by_z[j].astype(F32) + by_z[j + 4].astype(F32)
        encoded.append((at(x_tokens, (q - j) % 4, 1).astype(F32) + mixed).astype(BF))
    encoded = jnp.concatenate(encoded, axis=0)
    encoded_all = jnp.concatenate([encoded] + [ring(encoded, "mp", s) for s in (1, 2, 3)], axis=0)

    rolled = jnp.concatenate([kv_weight, kv_weight[:, :, : 3 * HD]], axis=2)
    rolled = lax.dynamic_slice_in_dim(rolled, q * HD, 4 * HD, 2)
    own_weight = rolled[:, :, :HD].reshape(width, 2 * HD)
    pair = jnp.dot(encoded_all, own_weight, preferred_element_type=F32).astype(BF)
    along_y = [pair] + [ring(pair, "dp", s) for s in (1, 2, 3)]
    pairs = along_y + [swap(part, "dp") for part in along_y]

    other_parts = [other] + [ring(other, "mp", s) for s in (1, 2, 3)]
    queries = jnp.zeros((3 * SPAN, 4 * HD), F32)
    for s in range(4):
        for flip, parts in ((0, own_parts), (1, other_parts)):
            m = (x - s) % 4 * 2 + (z_hi + flip) % 2
            rows = lax.dynamic_slice_in_dim(query_weight, m * 512, 512, 0)
            queries = queries + jnp.dot(parts[s], rows, preferred_element_type=F32)
    queries = queries.astype(BF).reshape(3, SPAN, 4, HD)
    head_parts = [at(queries, q, 2)] + [group_ring(at(queries, (q + s) % 4, 2), s) for s in (1, 2, 3)]
    head_parts = jnp.stack(head_parts)
    head_queries = jnp.concatenate([at(head_parts, (q - i) % 4) for i in range(4)], axis=1)

    back = [(i, i - 1) for i in range(1, 8)]
    grads = lax.dynamic_slice_in_dim(head_grads, q * HD, HD, 2)

    def window(value):
        following = lax.ppermute(value[:, :SPAN], "dp", back)
        moved = jnp.concatenate([value[:, SPAN - 1 :], following[:, : SPAN - 1]], axis=1)
        return moved.reshape(12, SPAN, HD)

    window_grads = window(grads)
    window_queries = window(head_queries)

    ids = lax.dynamic_slice_in_dim(neighbour_ids, dp * 4, 4, 1).reshape(12 * KNB)
    matches = ids[:, None] == jnp.arange(pool_slot.shape[0], dtype=jnp.int32)[None, :]
    slots = jnp.sum(jnp.where(matches, pool_slot[None, :], 0), axis=-1)
    owner, slot = slots // 4, slots % 4
    block = (owner + core) % 2 * 4 + (y - owner // 2) % 4
    table = jnp.stack([block, (q - slot) % 4], axis=1).astype(jnp.int32)

    grads_out = attention(table, window_queries, window_grads, pairs)

    mine, theirs = grads_out[:4], grads_out[4:]
    halves = {}
    for s in (2, 1, 3, 0):
        halves[s] = mine[s].astype(F32) + swap(theirs[s], "dp").astype(F32)
    slot_grads = halves[0]
    for s in (2, 1, 3):
        slot_grads = slot_grads + ring(halves[s].astype(BF), "dp", -s).astype(F32)
    slot_grads = slot_grads.astype(BF)

    by_slot = slot_grads.reshape(4, 4, 32, 2, HD)
    gathered = [by_slot[:, 0]] + [group_ring(by_slot[:, j], -j) for j in (1, 2, 3)]
    gathered = jnp.stack(gathered, axis=3).reshape(128, 2 * 4 * HD)
    returned = lax.dot_general(
        gathered, rolled.reshape(width, 8 * HD), (((1,), (1,)), ((), ())), preferred_element_type=F32
    )
    returned = returned.astype(BF).reshape(4, 32, width)
    x_sum = returned[0].astype(F32)
    for s in (2, 1, 3):
        x_sum = x_sum + ring(returned[s], "mp", -s).astype(F32)
    x_sum = x_sum.astype(BF).reshape(2, 16, width)
    z = z_hi * 4 + q
    z_parts = [at(x_sum, z_hi)] + [z_ring(at(x_sum, (z + s) % 8 // 4), s) for s in range(1, 8)]
    by_slot_sum = [z_parts[j].astype(F32) + z_parts[j + 4].astype(F32) for j in range(4)]
    by_slot_sum = jnp.stack(by_slot_sum)
    neighbour_grad = jnp.stack([at(by_slot_sum, (q - l) % 4) for l in range(4)], axis=1)

    weight_part = lax.dot_general(
        encoded_all, slot_grads, (((0,), (0,)), ((), ())), preferred_element_type=F32
    )
    weight_part = weight_part.astype(BF).reshape(4, 4, 2, 28, 2 * HD)
    half = at(weight_part, core, 2).astype(F32) + swap(at(weight_part, 1 - core, 2), "dp").astype(F32)
    sent = half.astype(BF)
    rows = at(half, y, 1)
    for s in (2, 1, 3):
        rows = rows + ring(at(sent, (y + s) % 4, 1), "dp", s).astype(F32)
    rows = rows.astype(BF)
    heads = [at(rows, q)] + [group_ring(at(rows, (q + s) % 4), s) for s in (1, 2, 3)]
    heads = jnp.stack(heads).reshape(4, 28, 2, HD)
    kv_grad = jnp.concatenate([at(heads, (q - h) % 4) for h in range(4)], axis=-1).astype(F32)
    return kv_grad, neighbour_grad


def solution(mesh):
    in_specs = (
        P(None, "dp", None),
        P(),
        P(None, "mp"),
        P("mp", None),
        P(None, "dp", "mp"),
        P(None, "dp", "mp"),
        P(None, "mp"),
        P(None, None, "mp"),
        P(),
        P(),
    )
    out_specs = (P(("grp", "dp"), None, "mp"), P("mp", "dp", None))
    return jax.shard_map(local, mesh=mesh, in_specs=in_specs, out_specs=out_specs, check_vma=False)
```

```python
import math

import jax
import jax.numpy as jnp
from jax import lax
from jax.experimental import pallas as pl
from jax.experimental.pallas import tpu as pltpu
from jax.sharding import PartitionSpec as P

HD = 128
SPAN = 64
KNB = 2
EPSILON = 1e-06
BF = jnp.bfloat16
F32 = jnp.float32


def ring(value, axis, by):
    return lax.ppermute(value, axis, [(i, (i // 2 + by) % 4 * 2 + i % 2) for i in range(8)])


def swap(value, axis):
    return lax.ppermute(value, axis, [(i, i ^ 1) for i in range(8)])


def group_ring(value, by):
    return lax.ppermute(value, "grp", [(i, (i + by) % 4) for i in range(4)])


def y_step(value, core0, core1):
    return lax.ppermute(
        value, "dp", [(i, (i // 2 + (core1 if i % 2 else core0)) % 4 * 2 + i % 2) for i in range(8)]
    )


def fence(*values):
    return lax.optimization_barrier(values)


def at(value, index, axis=0):
    return lax.dynamic_index_in_dim(value, index, axis, keepdims=False)


def encoder_partial(tokens, gain, up_cols, down_rows):
    values = tokens.astype(F32)
    inverse_rms = lax.rsqrt(jnp.mean(values * values, axis=-1, keepdims=True) + EPSILON)
    normed = (values * inverse_rms * gain).astype(BF)
    widened = jnp.dot(normed, up_cols, preferred_element_type=F32)
    widened = jax.nn.gelu(widened).astype(BF)
    return jnp.dot(widened, down_rows, preferred_element_type=F32)


def attention_kernel(table, queries, grads, *refs):
    own, near, pair_a, pair_b, far_a, far_b, mine, theirs, total, store = refs
    factor = 1.0 / math.sqrt(HD)
    total[...] = jnp.zeros_like(total)
    store[0] = own[...].reshape(4, 128, 2 * HD)
    store[1] = near[...].reshape(4, 128, 2 * HD)
    store[2:4] = pair_a[...].reshape(2, 4, 128, 2 * HD)
    store[4:6] = pair_b[...].reshape(2, 4, 128, 2 * HD)
    store[6] = far_a[...].reshape(4, 128, 2 * HD)
    store[7] = far_b[...].reshape(4, 128, 2 * HD)
    for span in range(12):
        where = []
        for k in range(KNB):
            where.append((table[span * KNB + k, 0], table[span * KNB + k, 1]))
        both = jnp.concatenate([store[b, s] for b, s in where], axis=0)
        keys, values = both[:, :HD], both[:, HD:]
        query = queries[span]
        grad = grads[span]
        nt = (((1,), (1,)), ((), ()))
        scores = lax.dot_general(keys, query, nt, preferred_element_type=F32) * factor
        weights = jnp.exp(scores - jnp.max(scores, axis=0, keepdims=True))
        probs = weights / jnp.sum(weights, axis=0, keepdims=True)
        value_grads = jnp.dot(probs.astype(BF), grad, preferred_element_type=F32)
        prob_grads = lax.dot_general(values, grad, nt, preferred_element_type=F32)
        inner = jnp.sum(probs * prob_grads, axis=0, keepdims=True)
        score_grads = (probs * (prob_grads - inner) * factor).astype(BF)
        key_grads = jnp.dot(score_grads, query, preferred_element_type=F32)
        for k, (b, s) in enumerate(where):
            rows = slice(k * 128, (k + 1) * 128)
            total[b, s, :, :HD] += key_grads[rows]
            total[b, s, :, HD:] += value_grads[rows]
    for out, blocks in ((mine, (0, 2, 5, 6)), (theirs, (1, 4, 3, 7))):
        for i, block in enumerate(blocks):
            out[i] = total[block].reshape(512, 2 * HD).astype(BF)


def attention(table, queries, grads, pairs):
    vmem = pl.BlockSpec(memory_space=pltpu.VMEM)
    return pl.pallas_call(
        attention_kernel,
        in_specs=[pl.BlockSpec(memory_space=pltpu.SMEM)] + [vmem] * 8,
        out_specs=[vmem] * 2,
        out_shape=[jax.ShapeDtypeStruct((4, 512, 2 * HD), BF)] * 2,
        scratch_shapes=[
            pltpu.VMEM((8, 4, 128, 2 * HD), F32),
            pltpu.VMEM((8, 4, 128, 2 * HD), BF),
        ],
        compiler_params=pltpu.CompilerParams(vmem_limit_bytes=32 * 1024 * 1024),
        cost_estimate=pl.CostEstimate(
            flops=12 * 5 * 2 * 64 * 256 * 128, bytes_accessed=5_000_000, transcendentals=12 * 64 * 256
        ),
        name="attention",
    )(table, queries, grads, *pairs)


def local(
    neighbour_tokens,
    enc_gain,
    enc_up,
    enc_down,
    hidden,
    head_grads,
    query_weight,
    kv_weight,
    neighbour_ids,
    pool_slot,
):
    q = lax.axis_index("grp")
    dp = lax.axis_index("dp")
    mp = lax.axis_index("mp")
    x, z_hi = mp // 2, mp % 2
    y, core = dp // 2, dp % 2
    width = neighbour_tokens.shape[-1]

    chunk = lax.dynamic_slice_in_dim(hidden, q * SPAN, SPAN, 1).reshape(3 * SPAN, -1)
    other = swap(chunk, "mp")
    own_parts = [chunk] + [ring(chunk, "mp", s) for s in (3, 2, 1)]
    own_tokens = at(neighbour_tokens, q, 1)
    partial = encoder_partial(own_tokens, enc_gain, enc_up, enc_down).astype(BF).reshape(4, 32, width)
    arrived = [ring(at(partial, (x + s) % 4), "mp", s) for s in (3, 2, 1)]
    own_share = lax.dynamic_slice_in_dim(own_tokens, x * 32, 32, 0).astype(F32)
    summed = at(partial, x).astype(F32) + own_share * 0.5
    for part in arrived:
        summed = summed + part.astype(F32)
    summed = summed.astype(BF)
    summed, other, own_parts, kv_weight, query_weight = fence(
        summed, other, own_parts, kv_weight, query_weight
    )

    other_parts = [other] + [ring(other, "mp", s) for s in (3, 2, 1)]
    encoded = (summed.astype(F32) + swap(summed, "mp").astype(F32)).astype(BF)
    encoded = jnp.stack([encoded] + [group_ring(encoded, s) for s in (1, 2, 3)])
    queries = jnp.zeros((3 * SPAN, 4 * HD), F32)
    for s, part in zip((0, 3, 2, 1), own_parts):
        rows = lax.dynamic_slice_in_dim(query_weight, ((x - s) % 4 * 2 + z_hi) * 512, 512, 0)
        queries = queries + jnp.dot(part, rows, preferred_element_type=F32)
    own_weight = lax.dynamic_slice_in_dim(kv_weight, q * HD, HD, 2).reshape(width, 2 * HD)
    encoded, other_parts, queries, query_weight, kv_weight, own_weight, head_grads = fence(
        encoded, other_parts, queries, query_weight, kv_weight, own_weight, head_grads
    )

    encoded_all = jnp.concatenate([encoded] + [ring(encoded, "mp", s) for s in (3, 2, 1)], axis=1)
    encoded_all = encoded_all.reshape(512, width)
    for s, part in zip((0, 3, 2, 1), other_parts):
        rows = lax.dynamic_slice_in_dim(query_weight, ((x - s) % 4 * 2 + 1 - z_hi) * 512, 512, 0)
        queries = queries + jnp.dot(part, rows, preferred_element_type=F32)
    queries = queries.astype(BF).reshape(3, SPAN, 4 * HD)

    def of_head(head):
        return lax.dynamic_slice_in_dim(queries, head * HD, HD, 2)

    head_parts = [of_head(q)] + [group_ring(of_head((q + s) % 4), s) for s in (1, 2, 3)]
    encoded_all, head_parts, own_weight, kv_weight = fence(
        encoded_all, head_parts, own_weight, kv_weight
    )

    pair = jnp.dot(encoded_all, own_weight, preferred_element_type=F32).astype(BF)
    far_a = y_step(pair, 2, 2)
    near = swap(pair, "dp")
    pair_a = y_step(jnp.stack([pair, near]), 1, -1)
    far_b = swap(far_a, "dp")
    pair_b = swap(pair_a, "dp")

    head_parts = jnp.stack(head_parts)
    head_queries = jnp.concatenate([at(head_parts, (q - i) % 4) for i in range(4)], axis=1)
    grads = lax.dynamic_slice_in_dim(head_grads, q * HD, HD, 2)
    both = jnp.concatenate([head_queries, grads], axis=0)
    following = lax.ppermute(both[:, :SPAN], "dp", [(i, i - 1) for i in range(1, 8)])
    moved = jnp.concatenate([both[:, SPAN - 1 :], following[:, : SPAN - 1]], axis=1)
    moved = moved.reshape(24, SPAN, HD)

    ids = lax.dynamic_slice_in_dim(neighbour_ids, dp * 4, 4, 1).reshape(12 * KNB)
    matches = ids[:, None] == jnp.arange(pool_slot.shape[0], dtype=jnp.int32)[None, :]
    slots = jnp.sum(jnp.where(matches, pool_slot[None, :], 0), axis=-1)
    owner, slot = slots // 4, slots % 4
    far, flip = (owner // 2 - y) % 4, (owner + core) % 2
    ahead = jnp.where(core == 0, 3, 1)
    block = jnp.where(far == ahead, 2 + flip, jnp.where(far % 2 == 1, 5 - flip, far * 3 + flip))
    table = jnp.stack([block, (q - slot) % 4], axis=1).astype(jnp.int32)

    rolled = jnp.concatenate(
        [lax.dynamic_slice_in_dim(kv_weight, (q + j) % 4 * HD, HD, 2).reshape(width, 2 * HD) for j in range(4)],
        axis=1,
    )
    moved, pairs, table, rolled = fence(
        moved, [pair, near, pair_a, pair_b, far_a, far_b], table, rolled
    )
    mine, theirs = attention(table, moved[:12], moved[12:], pairs)

    halves = mine.astype(F32) + swap(theirs, "dp").astype(F32)
    sent = halves.astype(BF)
    slot_grads = halves[0] + y_step(sent[3], 2, 2).astype(F32)
    slot_grads = slot_grads + y_step(sent[1], -1, 1).astype(F32) + y_step(sent[2], 1, -1).astype(F32)
    slot_grads = slot_grads.astype(BF)
    slot_grads, encoded_all, rolled = fence(slot_grads, encoded_all, rolled)

    by_slot = slot_grads.reshape(4, 128, 2 * HD)
    gathered = [by_slot[0]] + [group_ring(by_slot[j], -j) for j in (1, 2, 3)]
    weight_part = lax.dot_general(
        encoded_all, slot_grads, (((0,), (0,)), ((), ())), preferred_element_type=F32
    )
    weight_part = weight_part.astype(BF).reshape(4, 4, 2, 28, 2 * HD)
    kept, gone = at(weight_part, core, 2), at(weight_part, 1 - core, 2)
    half = kept.astype(F32) + swap(gone, "dp").astype(F32)
    sent = half.astype(BF)
    gathered = jnp.concatenate(gathered, axis=1)
    gathered, half, sent, rolled = fence(gathered, half, sent, rolled)

    returned = lax.dot_general(gathered, rolled, (((1,), (1,)), ((), ())), preferred_element_type=F32)
    returned = returned.astype(BF).reshape(4, 32, width)
    x_sum = returned[0].astype(F32)
    for i, s in ((1, 3), (2, 2), (3, 1)):
        x_sum = x_sum + ring(returned[i], "mp", -s).astype(F32)
    x_sum = x_sum.astype(BF).reshape(2, 16, width)
    rows = at(half, y, 1)
    for s in (3, 2, 1):
        rows = rows + ring(at(sent, (y + s) % 4, 1), "dp", s).astype(F32)
    rows = rows.astype(BF)
    x_sum, rows = fence(x_sum, rows)

    slot_sum = at(x_sum, z_hi).astype(F32) + swap(at(x_sum, 1 - z_hi), "mp").astype(F32)
    heads = [at(rows, q)] + [group_ring(at(rows, (q + s) % 4), s) for s in (1, 2, 3)]
    heads = jnp.stack(heads).reshape(4, 28, 2, HD)
    kv_grad = jnp.concatenate([at(heads, (q - h) % 4) for h in range(4)], axis=-1).astype(F32)
    slot_sum, kv_grad = fence(slot_sum, kv_grad)

    low = slot_sum.astype(BF)
    by_slot_sum = jnp.stack([low] + [group_ring(low, s) for s in (1, 2, 3)])
    neighbour_grad = jnp.stack([at(by_slot_sum, (q - l) % 4) for l in range(4)], axis=1).astype(F32)
    return kv_grad, neighbour_grad


def solution(mesh):
    in_specs = (
        P(None, "dp", None),
        P(),
        P(None, "mp"),
        P("mp", None),
        P(None, "dp", "mp"),
        P(None, "dp", "mp"),
        P(None, "mp"),
        P(None, None, "mp"),
        P(),
        P(),
    )
    out_specs = (P(("grp", "dp"), None, "mp"), P("mp", "dp", None))
    return jax.shard_map(local, mesh=mesh, in_specs=in_specs, out_specs=out_specs, check_vma=False)
```

```python
import math

import jax
import jax.numpy as jnp
from jax import lax
from jax.experimental import pallas as pl
from jax.experimental.pallas import tpu as pltpu
from jax.sharding import PartitionSpec as P

HD = 128
SPAN = 64
KNB = 2
EPSILON = 1e-06
BF = jnp.bfloat16
F32 = jnp.float32

AXES = ("grp", "y", "core", "x", "zhi")


def ring(value, axis, by):
    return lax.ppermute(value, axis, [(i, (i + by) % 4) for i in range(4)])


def swap(value, axis):
    return lax.ppermute(value, axis, [(0, 1), (1, 0)])


def fence(*values):
    return lax.optimization_barrier(values)


def at(value, index, axis=0):
    return lax.dynamic_index_in_dim(value, index, axis, keepdims=False)


def encoder_partial(tokens, gain, up_cols, down_rows):
    values = tokens.astype(F32)
    inverse_rms = lax.rsqrt(jnp.mean(values * values, axis=-1, keepdims=True) + EPSILON)
    normed = (values * inverse_rms * gain).astype(BF)
    widened = jnp.dot(normed, up_cols, preferred_element_type=F32)
    widened = jax.nn.gelu(widened).astype(BF)
    return jnp.dot(widened, down_rows, preferred_element_type=F32)


def attention_kernel(table, queries, grads, *refs):
    pairs, mine, theirs, total, store = refs[:8], refs[8], refs[9], refs[10], refs[11]
    factor = 1.0 / math.sqrt(HD)
    total[...] = jnp.zeros_like(total)
    for block in range(8):
        store[block] = pairs[block][...].reshape(4, 128, 2 * HD)
    for span in range(15):
        where = []
        for k in range(KNB):
            where.append((table[span * KNB + k, 0], table[span * KNB + k, 1]))
        both = jnp.concatenate([store[b, s] for b, s in where], axis=0)
        keys, values = both[:, :HD], both[:, HD:]
        query = queries[span]
        grad = grads[span]
        nt = (((1,), (1,)), ((), ()))
        scores = lax.dot_general(keys, query, nt, preferred_element_type=F32) * factor
        weights = jnp.exp(scores - jnp.max(scores, axis=0, keepdims=True))
        probs = weights / jnp.sum(weights, axis=0, keepdims=True)
        value_grads = jnp.dot(probs.astype(BF), grad, preferred_element_type=F32)
        prob_grads = lax.dot_general(values, grad, nt, preferred_element_type=F32)
        inner = jnp.sum(probs * prob_grads, axis=0, keepdims=True)
        score_grads = (probs * (prob_grads - inner) * factor).astype(BF)
        key_grads = jnp.dot(score_grads, query, preferred_element_type=F32)
        for k, (b, s) in enumerate(where):
            rows = slice(k * 128, (k + 1) * 128)
            total[b, s, :, :HD] += key_grads[rows]
            total[b, s, :, HD:] += value_grads[rows]
    for block in range(4):
        mine[block] = total[block].reshape(512, 2 * HD).astype(BF)
        theirs[block] = total[4 + block].reshape(512, 2 * HD).astype(BF)


def attention(table, queries, grads, pairs):
    vmem = pl.BlockSpec(memory_space=pltpu.VMEM)
    return pl.pallas_call(
        attention_kernel,
        in_specs=[pl.BlockSpec(memory_space=pltpu.SMEM)] + [vmem] * 10,
        out_specs=[vmem] * 2,
        out_shape=[jax.ShapeDtypeStruct((4, 512, 2 * HD), BF)] * 2,
        scratch_shapes=[
            pltpu.VMEM((8, 4, 128, 2 * HD), F32),
            pltpu.VMEM((8, 4, 128, 2 * HD), BF),
        ],
        compiler_params=pltpu.CompilerParams(vmem_limit_bytes=16 * 1024 * 1024),
        cost_estimate=pl.CostEstimate(
            flops=15 * 5 * 2 * 64 * 256 * 128, bytes_accessed=5_000_000, transcendentals=15 * 64 * 256
        ),
        name="attention",
    )(table, queries, grads, *pairs)


def project_kernel(places, *refs):
    parts, weight, before, out = refs[:4], refs[4], refs[5:-1], refs[-1]
    total = before[0][...] if before else jnp.zeros(out.shape, F32)
    for i in range(4):
        rows = pl.ds(pl.multiple_of(places[i] * 512, 512), 512)
        total += jnp.dot(parts[i][...], weight[rows, :], preferred_element_type=F32)
    out[...] = total.astype(out.dtype)


def project(places, parts, weight, before, dtype):
    vmem = pl.BlockSpec(memory_space=pltpu.VMEM)
    return pl.pallas_call(
        project_kernel,
        in_specs=[pl.BlockSpec(memory_space=pltpu.SMEM)] + [vmem] * (5 + len(before)),
        out_specs=vmem,
        out_shape=jax.ShapeDtypeStruct((3 * SPAN, 512), dtype),
        compiler_params=pltpu.CompilerParams(vmem_limit_bytes=12 * 1024 * 1024),
        cost_estimate=pl.CostEstimate(
            flops=2 * 192 * 2048 * 512, bytes_accessed=3_000_000, transcendentals=0
        ),
        name="project",
    )(places, *parts, weight, *before)


def local(
    neighbour_tokens,
    enc_gain,
    enc_up,
    enc_down,
    hidden,
    head_grads,
    query_weight,
    kv_weight,
    neighbour_ids,
    pool_slot,
):
    q = lax.axis_index("grp")
    y, core = lax.axis_index("y"), lax.axis_index("core")
    x, z_hi = lax.axis_index("x"), lax.axis_index("zhi")
    dp = y * 2 + core
    width = neighbour_tokens.shape[-1]

    chunk = lax.dynamic_slice_in_dim(hidden, q * SPAN, SPAN, 1).reshape(3 * SPAN, -1)
    other = swap(chunk, "zhi")
    own_tokens = at(neighbour_tokens, q, 1)
    partial = encoder_partial(own_tokens, enc_gain, enc_up, enc_down).astype(BF).reshape(4, 32, width)
    arrived = [ring(at(partial, (x + s) % 4), "x", s) for s in (3, 2, 1)]
    arrived[0], own_chunk = fence(arrived[0], chunk)
    own_parts = [chunk] + [ring(own_chunk, "x", s) for s in (1, 2, 3)]
    own_share = lax.dynamic_slice_in_dim(own_tokens, x * 32, 32, 0).astype(F32)
    summed = at(partial, x).astype(F32) + own_share * 0.5
    for part in arrived:
        summed = summed + part.astype(F32)
    summed, kv_weight, head_grads = fence(summed.astype(BF), kv_weight, head_grads)

    own_weight = lax.dynamic_slice_in_dim(kv_weight, q * HD, HD, 2).reshape(width, 2 * HD)
    encoded = (summed.astype(F32) + swap(summed, "zhi").astype(F32)).astype(BF)
    encoded, own_weight, other, own_parts = fence(encoded, own_weight, other, own_parts)

    encoded = jnp.stack([encoded] + [ring(encoded, "grp", s) for s in (1, 2, 3)])
    grads = lax.dynamic_slice_in_dim(head_grads, q * HD, HD, 2)
    encoded, own_weight, grads = fence(encoded, own_weight, grads)

    around = [encoded] + [ring(encoded, "x", s) for s in (1, 2, 3)]
    around[1], other = fence(around[1], other)
    other_parts = [other] + [ring(other, "x", s) for s in (1, 2, 3)]
    encoded_all = jnp.concatenate(around, axis=1).reshape(512, width)

    pair = jnp.dot(encoded_all, own_weight, preferred_element_type=F32).astype(BF)
    pair, own_parts, neighbour_ids = fence(pair, own_parts, neighbour_ids)
    pairs = [pair] + [ring(pair, "y", s) for s in (1, 2, 3)]

    places = jnp.stack([(x - s) % 4 * 2 for s in range(4)]).astype(jnp.int32)
    queries = project(places + z_hi, own_parts, query_weight, (), F32)
    queries = project(places + 1 - z_hi, other_parts, query_weight, (queries,), BF)
    queries = queries.reshape(3, SPAN, 4 * HD)

    def of_head(head):
        return lax.dynamic_slice_in_dim(queries, head * HD, HD, 2)

    head_parts = [of_head(q)] + [ring(of_head((q + s) % 4), "grp", s) for s in (1, 2, 3)]
    pairs += [swap(part, "core") for part in pairs]
    head_parts = jnp.stack(head_parts)
    head_queries = jnp.concatenate([at(head_parts, (q - i) % 4) for i in range(4)], axis=1)

    rows = jnp.arange(256, dtype=jnp.int32)[None, :, None]
    grads = jnp.where((dp > 0) | (rows >= SPAN - 1), grads, jnp.zeros_like(grads))

    def blocks(value):
        return jnp.pad(value, ((0, 0), (1, SPAN - 1), (0, 0))).reshape(15, SPAN, HD)

    head_queries, grads = blocks(head_queries), blocks(grads)

    ids = jnp.concatenate([neighbour_ids[:, :1], neighbour_ids], axis=1)
    ids = lax.dynamic_slice_in_dim(ids, dp * 4, 5, 1).reshape(15 * KNB)
    matches = ids[:, None] == jnp.arange(pool_slot.shape[0], dtype=jnp.int32)[None, :]
    slots = jnp.sum(jnp.where(matches, pool_slot[None, :], 0), axis=-1)
    owner, slot = slots // 4, slots % 4
    block = (owner + core) % 2 * 4 + (y - owner // 2) % 4
    table = jnp.stack([block, (q - slot) % 4], axis=1).astype(jnp.int32)

    head_queries, grads, pairs = fence(head_queries, grads, pairs)
    mine, theirs = attention(table, head_queries, grads, pairs)
    theirs, kv_weight = fence(theirs, kv_weight)
    rolled = jnp.concatenate(
        [lax.dynamic_slice_in_dim(kv_weight, (q + j) % 4 * HD, HD, 2).reshape(width, 2 * HD) for j in range(4)],
        axis=1,
    )

    halves = mine.astype(F32) + swap(theirs, "core").astype(F32)
    sent = halves.astype(BF)
    slot_grads = halves[0]
    for s in (1, 2, 3):
        slot_grads = slot_grads + ring(sent[s], "y", -s).astype(F32)
    slot_grads = slot_grads.astype(BF)
    slot_grads, encoded_all, rolled = fence(slot_grads, encoded_all, rolled)

    by_slot = slot_grads.reshape(4, 128, 2 * HD)
    gathered = [by_slot[0]] + [ring(by_slot[j], "grp", -j) for j in (1, 2, 3)]
    gathered[1], slot_grads = fence(gathered[1], slot_grads)
    weight_part = lax.dot_general(
        encoded_all, slot_grads, (((0,), (0,)), ((), ())), preferred_element_type=F32
    )
    weight_part = weight_part.astype(BF).reshape(4, 4, 2, 28, 2 * HD)
    gathered = jnp.concatenate(gathered, axis=1)
    gathered, weight_part, rolled = fence(gathered, weight_part, rolled)
    kept, gone = at(weight_part, core, 2), at(weight_part, 1 - core, 2)

    returned = lax.dot_general(gathered, rolled, (((1,), (1,)), ((), ())), preferred_element_type=F32)
    returned = returned.astype(BF).reshape(4, 32, width)
    half = kept.astype(F32) + swap(gone, "core").astype(F32)
    sent = half.astype(BF)
    x_sum = returned[0].astype(F32)
    for s in (1, 2, 3):
        x_sum = x_sum + ring(returned[s], "x", -s).astype(F32)
    x_sum = x_sum.astype(BF)
    rows = at(half, y, 1)
    for s in (3, 2, 1):
        rows = rows + ring(at(sent, (y + s) % 4, 1), "y", s).astype(F32)
    rows = rows.astype(BF)

    lanes = width // 128
    low = x_sum.reshape(2, 16, lanes, 128).transpose(0, 2, 1, 3).reshape(1, 2, lanes * 16, 128)
    low = jnp.broadcast_to(low, (4, 2, lanes * 16, 128))
    high = jnp.pad(rows, ((0, 0), (0, 4), (0, 0))).reshape(4, 32, 2, 128)
    high = high.transpose(0, 2, 1, 3).reshape(4, 1, 64, 128)
    high = jnp.broadcast_to(high, (4, 2, 64, 128))
    packed = jnp.concatenate([low, high], axis=2).reshape(8, lanes * 16 + 64, 128)
    (packed,) = fence(packed)
    packed = lax.all_to_all(packed, ("grp", "zhi"), 0, 0, tiled=True)
    packed = packed.reshape(4, 2, lanes * 16 + 64, 128)
    low = packed[:, :, : lanes * 16].astype(F32)
    low = (low[:, 0] + low[:, 1]).reshape(4, lanes, 16, 128)
    neighbour_grad = low.transpose(2, 0, 1, 3).reshape(16, 4, width)
    high = at(packed, z_hi, 1)[:, lanes * 16 :].reshape(4, 2, 32, 128)[:, :, :28]
    kv_grad = high.transpose(2, 1, 0, 3).reshape(28, 2, 4 * HD).astype(F32)
    return kv_grad, neighbour_grad


def solution(mesh):
    five = jax.sharding.Mesh(mesh.devices.reshape(4, 4, 2, 4, 2), AXES)
    dp, mp = ("y", "core"), ("x", "zhi")
    in_specs = (
        P(None, dp, None),
        P(),
        P(None, mp),
        P(mp, None),
        P(None, dp, mp),
        P(None, dp, mp),
        P(None, mp),
        P(None, None, mp),
        P(),
        P(),
    )
    out_specs = (P(("grp", "y", "core"), None, mp), P(mp, dp, None))
    return jax.shard_map(local, mesh=five, in_specs=in_specs, out_specs=out_specs, check_vma=False)
```

```python
import math

import jax
import jax.numpy as jnp
from jax import lax
from jax.experimental import pallas as pl
from jax.experimental.pallas import tpu as pltpu
from jax.sharding import PartitionSpec as P

HD = 128
SPAN = 64
KNB = 2
EPSILON = 1e-06
BF = jnp.bfloat16
F32 = jnp.float32

AXES = ("grp", "y", "core", "x", "zhi")


def ring(value, axis, by):
    return lax.ppermute(value, axis, [(i, (i + by) % 4) for i in range(4)])


def swap(value, axis):
    return lax.ppermute(value, axis, [(0, 1), (1, 0)])


def fence(*values):
    return lax.optimization_barrier(values)


def at(value, index, axis=0):
    return lax.dynamic_index_in_dim(value, index, axis, keepdims=False)


def encoder_partial(tokens, gain, up_cols, down_rows):
    values = tokens.astype(F32)
    inverse_rms = lax.rsqrt(jnp.mean(values * values, axis=-1, keepdims=True) + EPSILON)
    normed = (values * inverse_rms * gain).astype(BF)
    widened = jnp.dot(normed, up_cols, preferred_element_type=F32)
    widened = jax.nn.gelu(widened).astype(BF)
    return jnp.dot(widened, down_rows, preferred_element_type=F32)


def attention_kernel(table, queries, grads, *refs):
    pairs, mine, theirs, total, store = refs[:8], refs[8], refs[9], refs[10], refs[11]
    factor = 1.0 / math.sqrt(HD)
    total[...] = jnp.zeros_like(total)
    for block in range(8):
        store[block] = pairs[block][...].reshape(4, 128, 2 * HD)
    for span in range(15):
        where = []
        for k in range(KNB):
            where.append((table[span * KNB + k, 0], table[span * KNB + k, 1]))
        both = jnp.concatenate([store[b, s] for b, s in where], axis=0)
        keys, values = both[:, :HD], both[:, HD:]
        query = queries[span]
        grad = grads[span]
        nt = (((1,), (1,)), ((), ()))
        scores = lax.dot_general(keys, query, nt, preferred_element_type=F32) * factor
        weights = jnp.exp(scores - jnp.max(scores, axis=0, keepdims=True))
        probs = weights / jnp.sum(weights, axis=0, keepdims=True)
        value_grads = jnp.dot(probs.astype(BF), grad, preferred_element_type=F32)
        prob_grads = lax.dot_general(values, grad, nt, preferred_element_type=F32)
        inner = jnp.sum(probs * prob_grads, axis=0, keepdims=True)
        score_grads = (probs * (prob_grads - inner) * factor).astype(BF)
        key_grads = jnp.dot(score_grads, query, preferred_element_type=F32)
        for k, (b, s) in enumerate(where):
            rows = slice(k * 128, (k + 1) * 128)
            total[b, s, :, :HD] += key_grads[rows]
            total[b, s, :, HD:] += value_grads[rows]
    for block in range(4):
        mine[block] = total[block].reshape(512, 2 * HD).astype(BF)
        theirs[block] = total[4 + block].reshape(512, 2 * HD).astype(BF)


def attention(table, queries, grads, pairs):
    vmem = pl.BlockSpec(memory_space=pltpu.VMEM)
    return pl.pallas_call(
        attention_kernel,
        in_specs=[pl.BlockSpec(memory_space=pltpu.SMEM)] + [vmem] * 10,
        out_specs=[vmem] * 2,
        out_shape=[jax.ShapeDtypeStruct((4, 512, 2 * HD), BF)] * 2,
        scratch_shapes=[
            pltpu.VMEM((8, 4, 128, 2 * HD), F32),
            pltpu.VMEM((8, 4, 128, 2 * HD), BF),
        ],
        compiler_params=pltpu.CompilerParams(vmem_limit_bytes=16 * 1024 * 1024),
        cost_estimate=pl.CostEstimate(
            flops=15 * 5 * 2 * 64 * 256 * 128, bytes_accessed=5_000_000, transcendentals=15 * 64 * 256
        ),
        name="attention",
    )(table, queries, grads, *pairs)


def project_kernel(places, *refs):
    parts, weight, before, out = refs[:4], refs[4], refs[5:-1], refs[-1]
    total = before[0][...] if before else jnp.zeros(out.shape, F32)
    for i in range(4):
        rows = pl.ds(pl.multiple_of(places[i] * 512, 512), 512)
        total += jnp.dot(parts[i][...], weight[rows, :], preferred_element_type=F32)
    out[...] = total.astype(out.dtype)


def project(places, parts, weight, before, dtype):
    vmem = pl.BlockSpec(memory_space=pltpu.VMEM)
    return pl.pallas_call(
        project_kernel,
        in_specs=[pl.BlockSpec(memory_space=pltpu.SMEM)] + [vmem] * (5 + len(before)),
        out_specs=vmem,
        out_shape=jax.ShapeDtypeStruct((3 * SPAN, 512), dtype),
        compiler_params=pltpu.CompilerParams(vmem_limit_bytes=12 * 1024 * 1024),
        cost_estimate=pl.CostEstimate(
            flops=2 * 192 * 2048 * 512, bytes_accessed=3_000_000, transcendentals=0
        ),
        name="project",
    )(places, *parts, weight, *before)


def local(
    neighbour_tokens,
    enc_gain,
    enc_up,
    enc_down,
    hidden,
    head_grads,
    query_weight,
    kv_weight,
    neighbour_ids,
    pool_slot,
):
    q = lax.axis_index("grp")
    y, core = lax.axis_index("y"), lax.axis_index("core")
    x, z_hi = lax.axis_index("x"), lax.axis_index("zhi")
    dp = y * 2 + core
    width = neighbour_tokens.shape[-1]

    chunk = lax.dynamic_slice_in_dim(hidden, q * SPAN, SPAN, 1).reshape(3 * SPAN, -1)
    other = swap(chunk, "zhi")
    own_tokens = at(neighbour_tokens, q, 1)
    partial = encoder_partial(own_tokens, enc_gain, enc_up, enc_down).astype(BF).reshape(4, 32, width)
    arrived = [ring(at(partial, (x + s) % 4), "x", s) for s in (3, 2, 1)]
    arrived[0], own_chunk = fence(arrived[0], chunk)
    own_parts = [chunk] + [ring(own_chunk, "x", s) for s in (1, 2, 3)]
    own_share = lax.dynamic_slice_in_dim(own_tokens, x * 32, 32, 0).astype(F32)
    summed = at(partial, x).astype(F32) + own_share * 0.5
    for part in arrived:
        summed = summed + part.astype(F32)
    summed, kv_weight, head_grads = fence(summed.astype(BF), kv_weight, head_grads)

    own_weight = lax.dynamic_slice_in_dim(kv_weight, q * HD, HD, 2).reshape(width, 2 * HD)
    encoded = (summed.astype(F32) + swap(summed, "zhi").astype(F32)).astype(BF)
    encoded, own_weight, other, own_parts = fence(encoded, own_weight, other, own_parts)

    encoded = jnp.stack([encoded] + [ring(encoded, "grp", s) for s in (1, 2, 3)])
    grads = lax.dynamic_slice_in_dim(head_grads, q * HD, HD, 2)
    encoded, own_weight, grads, other = fence(encoded, own_weight, grads, other)

    around = [encoded] + [ring(encoded, "x", s) for s in (1, 2, 3)]
    other_parts = [other] + [ring(other, "x", s) for s in (1, 2, 3)]
    encoded_all = jnp.concatenate(around, axis=1).reshape(512, width)

    pair = jnp.dot(encoded_all, own_weight, preferred_element_type=F32).astype(BF)
    places = jnp.stack([(x - s) % 4 * 2 for s in range(4)]).astype(jnp.int32)
    queries = project(places + z_hi, own_parts, query_weight, (), F32)
    pair, queries, neighbour_ids = fence(pair, queries, neighbour_ids)
    pairs = [pair] + [ring(pair, "y", s) for s in (1, 2, 3)]

    queries = project(places + 1 - z_hi, other_parts, query_weight, (queries,), BF)
    queries = queries.reshape(3, SPAN, 4 * HD)

    def of_head(head):
        return lax.dynamic_slice_in_dim(queries, head * HD, HD, 2)

    head_parts = [of_head(q)] + [ring(of_head((q + s) % 4), "grp", s) for s in (1, 2, 3)]
    pairs += [swap(part, "core") for part in pairs]
    head_parts = jnp.stack(head_parts)
    head_queries = jnp.concatenate([at(head_parts, (q - i) % 4) for i in range(4)], axis=1)

    rows = jnp.arange(256, dtype=jnp.int32)[None, :, None]
    grads = jnp.where((dp > 0) | (rows >= SPAN - 1), grads, jnp.zeros_like(grads))

    def blocks(value):
        return jnp.pad(value, ((0, 0), (1, SPAN - 1), (0, 0))).reshape(15, SPAN, HD)

    head_queries, grads = blocks(head_queries), blocks(grads)

    ids = jnp.concatenate([neighbour_ids[:, :1], neighbour_ids], axis=1)
    ids = lax.dynamic_slice_in_dim(ids, dp * 4, 5, 1).reshape(15 * KNB)
    matches = ids[:, None] == jnp.arange(pool_slot.shape[0], dtype=jnp.int32)[None, :]
    slots = jnp.sum(jnp.where(matches, pool_slot[None, :], 0), axis=-1)
    owner, slot = slots // 4, slots % 4
    block = (owner + core) % 2 * 4 + (y - owner // 2) % 4
    table = jnp.stack([block, (q - slot) % 4], axis=1).astype(jnp.int32)

    head_queries, grads, pairs = fence(head_queries, grads, pairs)
    mine, theirs = attention(table, head_queries, grads, pairs)
    theirs, kv_weight = fence(theirs, kv_weight)
    rolled = jnp.concatenate(
        [lax.dynamic_slice_in_dim(kv_weight, (q + j) % 4 * HD, HD, 2).reshape(width, 2 * HD) for j in range(4)],
        axis=1,
    )

    halves = mine.astype(F32) + swap(theirs, "core").astype(F32)
    sent = halves.astype(BF)
    slot_grads = halves[0]
    for s in (1, 2, 3):
        slot_grads = slot_grads + ring(sent[s], "y", -s).astype(F32)
    slot_grads = slot_grads.astype(BF)
    slot_grads, encoded_all, rolled = fence(slot_grads, encoded_all, rolled)

    by_slot = slot_grads.reshape(4, 128, 2 * HD)
    gathered = [by_slot[0]] + [ring(by_slot[j], "grp", -j) for j in (1, 2, 3)]
    gathered[1], slot_grads = fence(gathered[1], slot_grads)
    weight_part = lax.dot_general(
        encoded_all, slot_grads, (((0,), (0,)), ((), ())), preferred_element_type=F32
    )
    weight_part = weight_part.astype(BF).reshape(4, 4, 2, 28, 2 * HD)
    gathered = jnp.concatenate(gathered, axis=1)
    gathered, weight_part, rolled = fence(gathered, weight_part, rolled)
    kept, gone = at(weight_part, core, 2), at(weight_part, 1 - core, 2)

    returned = lax.dot_general(gathered, rolled, (((1,), (1,)), ((), ())), preferred_element_type=F32)
    returned = returned.astype(BF).reshape(4, 32, width)
    half = kept.astype(F32) + swap(gone, "core").astype(F32)
    sent = half.astype(BF)
    x_sum = returned[0].astype(F32)
    for s in (1, 2, 3):
        x_sum = x_sum + ring(returned[s], "x", -s).astype(F32)
    x_sum = x_sum.astype(BF)
    rows = at(half, y, 1)
    for s in (3, 2, 1):
        rows = rows + ring(at(sent, (y + s) % 4, 1), "y", s).astype(F32)
    rows = rows.astype(BF)

    halves = x_sum.reshape(2, 16, width)
    low = at(halves, z_hi).astype(F32) + swap(at(halves, 1 - z_hi), "zhi").astype(F32)
    lanes = width // 128
    low = low.astype(BF).reshape(16, lanes, 128).transpose(1, 0, 2).reshape(lanes * 16, 128)
    high = jnp.pad(rows, ((0, 0), (0, 4), (0, 0))).reshape(4, 32, 2, 128)
    high = high.transpose(0, 2, 1, 3).reshape(4, 64, 128)
    packed = [jnp.concatenate([low, at(high, (q + s) % 4)], axis=0) for s in range(4)]
    packed = jnp.stack([packed[0]] + [ring(packed[s], "grp", s) for s in (1, 2, 3)])
    packed = jnp.stack([at(packed, (q - s) % 4) for s in range(4)])
    low = packed[:, : lanes * 16].reshape(4, lanes, 16, 128)
    neighbour_grad = low.transpose(2, 0, 1, 3).reshape(16, 4, width).astype(F32)
    high = packed[:, lanes * 16 :].reshape(4, 2, 32, 128)[:, :, :28]
    kv_grad = high.transpose(2, 1, 0, 3).reshape(28, 2, 4 * HD).astype(F32)
    return kv_grad, neighbour_grad


def solution(mesh):
    five = jax.sharding.Mesh(mesh.devices.reshape(4, 4, 2, 4, 2), AXES)
    dp, mp = ("y", "core"), ("x", "zhi")
    in_specs = (
        P(None, dp, None),
        P(),
        P(None, mp),
        P(mp, None),
        P(None, dp, mp),
        P(None, dp, mp),
        P(None, mp),
        P(None, None, mp),
        P(),
        P(),
    )
    out_specs = (P(("grp", "y", "core"), None, mp), P(mp, dp, None))
    return jax.shard_map(local, mesh=five, in_specs=in_specs, out_specs=out_specs, check_vma=False)
```

```python
import math

import jax
import jax.numpy as jnp
from jax import lax
from jax.experimental import pallas as pl
from jax.experimental.pallas import tpu as pltpu
from jax.sharding import PartitionSpec as P

HD = 128
SPAN = 64
KNB = 2
EPSILON = 1e-06
BF = jnp.bfloat16
F32 = jnp.float32

AXES = ("grp", "y", "core", "x", "zhi")


def ring(value, axis, by):
    return lax.ppermute(value, axis, [(i, (i + by) % 4) for i in range(4)])


def swap(value, axis):
    return lax.ppermute(value, axis, [(0, 1), (1, 0)])


def fence(*values):
    return lax.optimization_barrier(values)


def at(value, index, axis=0):
    return lax.dynamic_index_in_dim(value, index, axis, keepdims=False)


def encoder_partial(tokens, gain, up_cols, down_rows):
    values = tokens.astype(F32)
    inverse_rms = lax.rsqrt(jnp.mean(values * values, axis=-1, keepdims=True) + EPSILON)
    normed = (values * inverse_rms * gain).astype(BF)
    widened = jnp.dot(normed, up_cols, preferred_element_type=F32)
    widened = jax.nn.gelu(widened).astype(BF)
    return jnp.dot(widened, down_rows, preferred_element_type=F32)


def attention_kernel(table, queries, grads, *refs):
    pairs, mine, theirs, total, store = refs[:8], refs[8], refs[9], refs[10], refs[11]
    factor = 1.0 / math.sqrt(HD)
    total[...] = jnp.zeros_like(total)
    for block in range(8):
        store[block] = pairs[block][...].reshape(4, 128, 2 * HD)
    for span in range(15):
        where = []
        for k in range(KNB):
            where.append((table[span * KNB + k, 0], table[span * KNB + k, 1]))
        both = jnp.concatenate([store[b, s] for b, s in where], axis=0)
        keys, values = both[:, :HD], both[:, HD:]
        query = queries[span]
        grad = grads[span]
        nt = (((1,), (1,)), ((), ()))
        scores = lax.dot_general(keys, query, nt, preferred_element_type=F32) * factor
        weights = jnp.exp(scores - jnp.max(scores, axis=0, keepdims=True))
        probs = weights / jnp.sum(weights, axis=0, keepdims=True)
        value_grads = jnp.dot(probs.astype(BF), grad, preferred_element_type=F32)
        prob_grads = lax.dot_general(values, grad, nt, preferred_element_type=F32)
        inner = jnp.sum(probs * prob_grads, axis=0, keepdims=True)
        score_grads = (probs * (prob_grads - inner) * factor).astype(BF)
        key_grads = jnp.dot(score_grads, query, preferred_element_type=F32)
        for k, (b, s) in enumerate(where):
            rows = slice(k * 128, (k + 1) * 128)
            total[b, s, :, :HD] += key_grads[rows]
            total[b, s, :, HD:] += value_grads[rows]
    for block in range(4):
        mine[block] = total[block].reshape(512, 2 * HD).astype(BF)
        theirs[block] = total[4 + block].reshape(512, 2 * HD).astype(BF)


def attention(table, queries, grads, pairs):
    vmem = pl.BlockSpec(memory_space=pltpu.VMEM)
    return pl.pallas_call(
        attention_kernel,
        in_specs=[pl.BlockSpec(memory_space=pltpu.SMEM)] + [vmem] * 10,
        out_specs=[vmem] * 2,
        out_shape=[jax.ShapeDtypeStruct((4, 512, 2 * HD), BF)] * 2,
        scratch_shapes=[
            pltpu.VMEM((8, 4, 128, 2 * HD), F32),
            pltpu.VMEM((8, 4, 128, 2 * HD), BF),
        ],
        compiler_params=pltpu.CompilerParams(vmem_limit_bytes=16 * 1024 * 1024),
        cost_estimate=pl.CostEstimate(
            flops=15 * 5 * 2 * 64 * 256 * 128, bytes_accessed=5_000_000, transcendentals=15 * 64 * 256
        ),
        name="attention",
    )(table, queries, grads, *pairs)


def project_kernel(places, *refs):
    parts, weight, before, out = refs[:4], refs[4], refs[5:-1], refs[-1]
    total = before[0][...] if before else jnp.zeros(out.shape, F32)
    for i in range(4):
        rows = pl.ds(pl.multiple_of(places[i] * 512, 512), 512)
        total += jnp.dot(parts[i][...], weight[rows, :], preferred_element_type=F32)
    out[...] = total.astype(out.dtype)


def project(places, parts, weight, before, dtype):
    vmem = pl.BlockSpec(memory_space=pltpu.VMEM)
    return pl.pallas_call(
        project_kernel,
        in_specs=[pl.BlockSpec(memory_space=pltpu.SMEM)] + [vmem] * (5 + len(before)),
        out_specs=vmem,
        out_shape=jax.ShapeDtypeStruct((3 * SPAN, 512), dtype),
        compiler_params=pltpu.CompilerParams(vmem_limit_bytes=12 * 1024 * 1024),
        cost_estimate=pl.CostEstimate(
            flops=2 * 192 * 2048 * 512, bytes_accessed=3_000_000, transcendentals=0
        ),
        name="project",
    )(places, *parts, weight, *before)


def local(
    neighbour_tokens,
    enc_gain,
    enc_up,
    enc_down,
    hidden,
    head_grads,
    query_weight,
    kv_weight,
    neighbour_ids,
    pool_slot,
):
    q = lax.axis_index("grp")
    y, core = lax.axis_index("y"), lax.axis_index("core")
    x, z_hi = lax.axis_index("x"), lax.axis_index("zhi")
    dp = y * 2 + core
    width = neighbour_tokens.shape[-1]

    chunk = lax.dynamic_slice_in_dim(hidden, q * SPAN, SPAN, 1).reshape(3 * SPAN, -1)
    other = swap(chunk, "zhi")
    own_tokens = at(neighbour_tokens, q, 1)
    partial = encoder_partial(own_tokens, enc_gain, enc_up, enc_down).astype(BF).reshape(4, 32, width)
    arrived = [ring(at(partial, (x + s) % 4), "x", s) for s in (3, 2, 1)]
    arrived[0], own_chunk = fence(arrived[0], chunk)
    own_parts = [chunk] + [ring(own_chunk, "x", s) for s in (1, 2, 3)]
    own_share = lax.dynamic_slice_in_dim(own_tokens, x * 32, 32, 0).astype(F32)
    summed = at(partial, x).astype(F32) + own_share * 0.5
    for part in arrived:
        summed = summed + part.astype(F32)
    summed, kv_weight, head_grads = fence(summed.astype(BF), kv_weight, head_grads)

    own_weight = lax.dynamic_slice_in_dim(kv_weight, q * HD, HD, 2).reshape(width, 2 * HD)
    encoded = (summed.astype(F32) + swap(summed, "zhi").astype(F32)).astype(BF)
    encoded, own_weight, other, own_parts = fence(encoded, own_weight, other, own_parts)

    encoded = jnp.stack([encoded] + [ring(encoded, "grp", s) for s in (1, 2, 3)])
    grads = lax.dynamic_slice_in_dim(head_grads, q * HD, HD, 2)
    encoded, own_weight, grads, other = fence(encoded, own_weight, grads, other)

    around = [encoded] + [ring(encoded, "x", s) for s in (1, 2, 3)]
    other_parts = [other] + [ring(other, "x", s) for s in (1, 2, 3)]
    encoded_all = jnp.concatenate(around, axis=1).reshape(512, width)

    pair = jnp.dot(encoded_all, own_weight, preferred_element_type=F32).astype(BF)
    places = jnp.stack([(x - s) % 4 * 2 for s in range(4)]).astype(jnp.int32)
    queries = project(places + z_hi, own_parts, query_weight, (), F32)
    pair, queries, neighbour_ids = fence(pair, queries, neighbour_ids)
    pairs = [pair] + [ring(pair, "y", s) for s in (1, 2, 3)]

    queries = project(places + 1 - z_hi, other_parts, query_weight, (queries,), BF)
    queries = queries.reshape(3, SPAN, 4 * HD)

    def of_head(head):
        return lax.dynamic_slice_in_dim(queries, head * HD, HD, 2)

    head_parts = [of_head(q)] + [ring(of_head((q + s) % 4), "grp", s) for s in (1, 2, 3)]
    pairs += [swap(part, "core") for part in pairs]
    head_parts = jnp.stack(head_parts)
    head_queries = jnp.concatenate([at(head_parts, (q - i) % 4) for i in range(4)], axis=1)

    rows = jnp.arange(256, dtype=jnp.int32)[None, :, None]
    grads = jnp.where((dp > 0) | (rows >= SPAN - 1), grads, jnp.zeros_like(grads))

    def blocks(value):
        return jnp.pad(value, ((0, 0), (1, SPAN - 1), (0, 0))).reshape(15, SPAN, HD)

    head_queries, grads = blocks(head_queries), blocks(grads)

    ids = jnp.concatenate([neighbour_ids[:, :1], neighbour_ids], axis=1)
    ids = lax.dynamic_slice_in_dim(ids, dp * 4, 5, 1).reshape(15 * KNB)
    matches = ids[:, None] == jnp.arange(pool_slot.shape[0], dtype=jnp.int32)[None, :]
    slots = jnp.sum(jnp.where(matches, pool_slot[None, :], 0), axis=-1)
    owner, slot = slots // 4, slots % 4
    block = (owner + core) % 2 * 4 + (y - owner // 2) % 4
    table = jnp.stack([block, (q - slot) % 4], axis=1).astype(jnp.int32)

    head_queries, grads, pairs = fence(head_queries, grads, pairs)
    mine, theirs = attention(table, head_queries, grads, pairs)
    theirs, kv_weight = fence(theirs, kv_weight)
    rolled = jnp.concatenate(
        [lax.dynamic_slice_in_dim(kv_weight, (q + j) % 4 * HD, HD, 2).reshape(width, 2 * HD) for j in range(4)],
        axis=1,
    )

    halves = mine.astype(F32) + swap(theirs, "core").astype(F32)
    sent = halves.astype(BF)
    slot_grads = halves[0]
    for s in (1, 2, 3):
        slot_grads = slot_grads + ring(sent[s], "y", -s).astype(F32)
    slot_grads = slot_grads.astype(BF)
    slot_grads, encoded_all, rolled = fence(slot_grads, encoded_all, rolled)

    by_slot = slot_grads.reshape(4, 128, 2 * HD)
    gathered = [by_slot[0]] + [ring(by_slot[j], "grp", -j) for j in (1, 2, 3)]
    gathered = jnp.concatenate(gathered, axis=1)
    returned = lax.dot_general(gathered, rolled, (((1,), (1,)), ((), ())), preferred_element_type=F32)
    returned = returned.astype(BF).reshape(4, 32, width)
    arrived = [ring(returned[s], "x", -s) for s in (1, 2, 3)]
    x_sum = returned[0].astype(F32)

    arrived[0], slot_grads, encoded_all = fence(arrived[0], slot_grads, encoded_all)
    for part in arrived:
        x_sum = x_sum + part.astype(F32)
    x_sum = x_sum.astype(BF)
    weight_part = lax.dot_general(
        encoded_all, slot_grads, (((0,), (0,)), ((), ())), preferred_element_type=F32
    )
    weight_part = weight_part.astype(BF).reshape(4, 4, 2, 28, 2 * HD)
    kept, gone = at(weight_part, core, 2), at(weight_part, 1 - core, 2)
    half = kept.astype(F32) + swap(gone, "core").astype(F32)
    sent = half.astype(BF)
    rows = at(half, y, 1)
    for s in (3, 2, 1):
        rows = rows + ring(at(sent, (y + s) % 4, 1), "y", s).astype(F32)
    rows = rows.astype(BF)

    halves = x_sum.reshape(2, 16, width)
    low = at(halves, z_hi).astype(F32) + swap(at(halves, 1 - z_hi), "zhi").astype(F32)
    lanes = width // 128
    low = low.astype(BF).reshape(16, lanes, 128).transpose(1, 0, 2).reshape(lanes * 16, 128)
    high = jnp.pad(rows, ((0, 0), (0, 4), (0, 0))).reshape(4, 32, 2, 128)
    high = high.transpose(0, 2, 1, 3).reshape(4, 64, 128)
    packed = [jnp.concatenate([low, at(high, (q + s) % 4)], axis=0) for s in range(4)]
    packed = jnp.stack([packed[0]] + [ring(packed[s], "grp", s) for s in (1, 2, 3)])
    packed = jnp.stack([at(packed, (q - s) % 4) for s in range(4)])
    low = packed[:, : lanes * 16].reshape(4, lanes, 16, 128)
    neighbour_grad = low.transpose(2, 0, 1, 3).reshape(16, 4, width).astype(F32)
    high = packed[:, lanes * 16 :].reshape(4, 2, 32, 128)[:, :, :28]
    kv_grad = high.transpose(2, 1, 0, 3).reshape(28, 2, 4 * HD).astype(F32)
    return kv_grad, neighbour_grad


def solution(mesh):
    five = jax.sharding.Mesh(mesh.devices.reshape(4, 4, 2, 4, 2), AXES)
    dp, mp = ("y", "core"), ("x", "zhi")
    in_specs = (
        P(None, dp, None),
        P(),
        P(None, mp),
        P(mp, None),
        P(None, dp, mp),
        P(None, dp, mp),
        P(None, mp),
        P(None, None, mp),
        P(),
        P(),
    )
    out_specs = (P(("grp", "y", "core"), None, mp), P(mp, dp, None))
    return jax.shard_map(local, mesh=five, in_specs=in_specs, out_specs=out_specs, check_vma=False)
```

```python
import math

import jax
import jax.numpy as jnp
from jax import lax
from jax.experimental import pallas as pl
from jax.experimental.pallas import tpu as pltpu
from jax.sharding import PartitionSpec as P

HD = 128
SPAN = 64
KNB = 2
EPSILON = 1e-06
BF = jnp.bfloat16
F32 = jnp.float32

AXES = ("grp", "y", "core", "x", "zhi")


def ring(value, axis, by):
    return lax.ppermute(value, axis, [(i, (i + by) % 4) for i in range(4)])


def swap(value, axis):
    return lax.ppermute(value, axis, [(0, 1), (1, 0)])


def fence(*values):
    return lax.optimization_barrier(values)


def at(value, index, axis=0):
    return lax.dynamic_index_in_dim(value, index, axis, keepdims=False)


def encoder_partial(tokens, gain, up_cols, down_rows):
    values = tokens.astype(F32)
    inverse_rms = lax.rsqrt(jnp.mean(values * values, axis=-1, keepdims=True) + EPSILON)
    normed = (values * inverse_rms * gain).astype(BF)
    widened = jnp.dot(normed, up_cols, preferred_element_type=F32)
    widened = jax.nn.gelu(widened).astype(BF)
    return jnp.dot(widened, down_rows, preferred_element_type=F32)


def attention_kernel(table, queries, grads, *refs):
    pairs, mine, theirs, total, store = refs[:8], refs[8], refs[9], refs[10], refs[11]
    factor = 1.0 / math.sqrt(HD)
    total[...] = jnp.zeros_like(total)
    for block in range(8):
        store[block] = pairs[block][...].reshape(4, 128, 2 * HD)
    for span in range(15):
        where = []
        for k in range(KNB):
            where.append((table[span * KNB + k, 0], table[span * KNB + k, 1]))
        both = jnp.concatenate([store[b, s] for b, s in where], axis=0)
        keys, values = both[:, :HD], both[:, HD:]
        query = queries[span]
        grad = grads[span]
        nt = (((1,), (1,)), ((), ()))
        scores = lax.dot_general(keys, query, nt, preferred_element_type=F32) * factor
        weights = jnp.exp(scores - jnp.max(scores, axis=0, keepdims=True))
        probs = weights / jnp.sum(weights, axis=0, keepdims=True)
        value_grads = jnp.dot(probs.astype(BF), grad, preferred_element_type=F32)
        prob_grads = lax.dot_general(values, grad, nt, preferred_element_type=F32)
        inner = jnp.sum(probs * prob_grads, axis=0, keepdims=True)
        score_grads = (probs * (prob_grads - inner) * factor).astype(BF)
        key_grads = jnp.dot(score_grads, query, preferred_element_type=F32)
        for k, (b, s) in enumerate(where):
            rows = slice(k * 128, (k + 1) * 128)
            total[b, s, :, :HD] += key_grads[rows]
            total[b, s, :, HD:] += value_grads[rows]
    for block in range(4):
        mine[block] = total[block].reshape(512, 2 * HD).astype(BF)
        theirs[block] = total[4 + block].reshape(512, 2 * HD).astype(BF)


def attention(table, queries, grads, pairs):
    vmem = pl.BlockSpec(memory_space=pltpu.VMEM)
    return pl.pallas_call(
        attention_kernel,
        in_specs=[pl.BlockSpec(memory_space=pltpu.SMEM)] + [vmem] * 10,
        out_specs=[vmem] * 2,
        out_shape=[jax.ShapeDtypeStruct((4, 512, 2 * HD), BF)] * 2,
        scratch_shapes=[
            pltpu.VMEM((8, 4, 128, 2 * HD), F32),
            pltpu.VMEM((8, 4, 128, 2 * HD), BF),
        ],
        compiler_params=pltpu.CompilerParams(vmem_limit_bytes=16 * 1024 * 1024),
        cost_estimate=pl.CostEstimate(
            flops=15 * 5 * 2 * 64 * 256 * 128, bytes_accessed=5_000_000, transcendentals=15 * 64 * 256
        ),
        name="attention",
    )(table, queries, grads, *pairs)


def project_kernel(places, *refs):
    parts, weight, before, out = refs[:4], refs[4], refs[5:-1], refs[-1]
    total = before[0][...] if before else jnp.zeros(out.shape, F32)
    for i in range(4):
        rows = pl.ds(pl.multiple_of(places[i] * 512, 512), 512)
        total += jnp.dot(parts[i][...], weight[rows, :], preferred_element_type=F32)
    out[...] = total.astype(out.dtype)


def project(places, parts, weight, before, dtype):
    vmem = pl.BlockSpec(memory_space=pltpu.VMEM)
    return pl.pallas_call(
        project_kernel,
        in_specs=[pl.BlockSpec(memory_space=pltpu.SMEM)] + [vmem] * (5 + len(before)),
        out_specs=vmem,
        out_shape=jax.ShapeDtypeStruct((3 * SPAN, 512), dtype),
        compiler_params=pltpu.CompilerParams(vmem_limit_bytes=12 * 1024 * 1024),
        cost_estimate=pl.CostEstimate(
            flops=2 * 192 * 2048 * 512, bytes_accessed=3_000_000, transcendentals=0
        ),
        name="project",
    )(places, *parts, weight, *before)


def local(
    neighbour_tokens,
    enc_gain,
    enc_up,
    enc_down,
    hidden,
    head_grads,
    query_weight,
    kv_weight,
    neighbour_ids,
    pool_slot,
):
    q = lax.axis_index("grp")
    y, core = lax.axis_index("y"), lax.axis_index("core")
    x, z_hi = lax.axis_index("x"), lax.axis_index("zhi")
    dp = y * 2 + core
    width = neighbour_tokens.shape[-1]

    chunk = lax.dynamic_slice_in_dim(hidden, q * SPAN, SPAN, 1).reshape(3 * SPAN, -1)
    other = swap(chunk, "zhi")
    own_tokens = at(neighbour_tokens, q, 1)
    partial = encoder_partial(own_tokens, enc_gain, enc_up, enc_down).astype(BF).reshape(4, 32, width)
    arrived = [ring(at(partial, (x + s) % 4), "x", s) for s in (3, 2, 1)]
    arrived[0], own_chunk = fence(arrived[0], chunk)
    own_parts = [chunk] + [ring(own_chunk, "x", s) for s in (1, 2, 3)]
    own_share = lax.dynamic_slice_in_dim(own_tokens, x * 32, 32, 0).astype(F32)
    summed = at(partial, x).astype(F32) + own_share * 0.5
    for part in arrived:
        summed = summed + part.astype(F32)
    summed, kv_weight, head_grads = fence(summed.astype(BF), kv_weight, head_grads)

    own_weight = lax.dynamic_slice_in_dim(kv_weight, q * HD, HD, 2).reshape(width, 2 * HD)
    encoded = (summed.astype(F32) + swap(summed, "zhi").astype(F32)).astype(BF)
    encoded, own_weight, other, own_parts = fence(encoded, own_weight, other, own_parts)

    encoded = jnp.stack([encoded] + [ring(encoded, "grp", s) for s in (1, 2, 3)])
    grads = lax.dynamic_slice_in_dim(head_grads, q * HD, HD, 2)
    encoded, own_weight, grads, other, own_parts = fence(encoded, own_weight, grads, other, own_parts)

    around = [encoded] + [ring(encoded, "x", s) for s in (1, 2, 3)]
    other_parts = [other] + [ring(other, "x", s) for s in (1, 2, 3)]
    encoded_all = jnp.concatenate(around, axis=1).reshape(512, width)

    pair = jnp.dot(encoded_all, own_weight, preferred_element_type=F32).astype(BF)
    places = jnp.stack([(x - s) % 4 * 2 for s in range(4)]).astype(jnp.int32)
    queries = project(places + z_hi, own_parts, query_weight, (), F32)
    pair, queries, neighbour_ids = fence(pair, queries, neighbour_ids)
    pairs = [pair] + [ring(pair, "y", s) for s in (1, 2, 3)]

    queries = project(places + 1 - z_hi, other_parts, query_weight, (queries,), BF)
    queries = queries.reshape(3, SPAN, 4 * HD)

    def of_head(head):
        return lax.dynamic_slice_in_dim(queries, head * HD, HD, 2)

    head_parts = [of_head(q)] + [ring(of_head((q + s) % 4), "grp", s) for s in (1, 2, 3)]
    pairs += [swap(part, "core") for part in pairs]
    head_parts = jnp.stack(head_parts)
    head_queries = jnp.concatenate([at(head_parts, (q - i) % 4) for i in range(4)], axis=1)

    rows = jnp.arange(256, dtype=jnp.int32)[None, :, None]
    grads = jnp.where((dp > 0) | (rows >= SPAN - 1), grads, jnp.zeros_like(grads))

    def blocks(value):
        return jnp.pad(value, ((0, 0), (1, SPAN - 1), (0, 0))).reshape(15, SPAN, HD)

    head_queries, grads = blocks(head_queries), blocks(grads)

    ids = jnp.concatenate([neighbour_ids[:, :1], neighbour_ids], axis=1)
    ids = lax.dynamic_slice_in_dim(ids, dp * 4, 5, 1).reshape(15 * KNB)
    matches = ids[:, None] == jnp.arange(pool_slot.shape[0], dtype=jnp.int32)[None, :]
    slots = jnp.sum(jnp.where(matches, pool_slot[None, :], 0), axis=-1)
    owner, slot = slots // 4, slots % 4
    block = (owner + core) % 2 * 4 + (y - owner // 2) % 4
    table = jnp.stack([block, (q - slot) % 4], axis=1).astype(jnp.int32)

    head_queries, grads, pairs = fence(head_queries, grads, pairs)
    mine, theirs = attention(table, head_queries, grads, pairs)
    theirs, kv_weight = fence(theirs, kv_weight)
    rolled = jnp.concatenate(
        [lax.dynamic_slice_in_dim(kv_weight, (q + j) % 4 * HD, HD, 2).reshape(width, 2 * HD) for j in range(4)],
        axis=1,
    )

    halves = mine.astype(F32) + swap(theirs, "core").astype(F32)
    sent = halves.astype(BF)
    slot_grads = halves[0]
    for s in (1, 2, 3):
        slot_grads = slot_grads + ring(sent[s], "y", -s).astype(F32)
    slot_grads = slot_grads.astype(BF)
    slot_grads, encoded_all, rolled = fence(slot_grads, encoded_all, rolled)

    by_slot = slot_grads.reshape(4, 128, 2 * HD)
    gathered = [by_slot[0]] + [ring(by_slot[j], "grp", -j) for j in (1, 2, 3)]
    gathered = jnp.concatenate(gathered, axis=1)
    returned = lax.dot_general(gathered, rolled, (((1,), (1,)), ((), ())), preferred_element_type=F32)
    returned = returned.astype(BF).reshape(4, 32, width)
    arrived = [ring(returned[s], "x", -s) for s in (1, 2, 3)]
    x_sum = returned[0].astype(F32)

    arrived[0], slot_grads, encoded_all = fence(arrived[0], slot_grads, encoded_all)
    for part in arrived:
        x_sum = x_sum + part.astype(F32)
    x_sum = x_sum.astype(BF)
    weight_part = lax.dot_general(
        encoded_all, slot_grads, (((0,), (0,)), ((), ())), preferred_element_type=F32
    )
    weight_part = weight_part.astype(BF).reshape(4, 4, 2, 28, 2 * HD)
    kept, gone = at(weight_part, core, 2), at(weight_part, 1 - core, 2)
    half = kept.astype(F32) + swap(gone, "core").astype(F32)
    sent = half.astype(BF)
    rows = at(half, y, 1)
    for s in (3, 2, 1):
        rows = rows + ring(at(sent, (y + s) % 4, 1), "y", s).astype(F32)
    rows = rows.astype(BF)

    halves = x_sum.reshape(2, 16, width)
    low = at(halves, z_hi).astype(F32) + swap(at(halves, 1 - z_hi), "zhi").astype(F32)
    lanes = width // 128
    low = low.astype(BF).reshape(16, lanes, 128).transpose(1, 0, 2).reshape(lanes * 16, 128)
    high = jnp.pad(rows, ((0, 0), (0, 4), (0, 0))).reshape(4, 32, 2, 128)
    high = high.transpose(0, 2, 1, 3).reshape(4, 64, 128)
    packed = [jnp.concatenate([low, at(high, (q + s) % 4)], axis=0) for s in range(4)]
    packed = jnp.stack([packed[0]] + [ring(packed[s], "grp", s) for s in (1, 2, 3)])
    packed = jnp.stack([at(packed, (q - s) % 4) for s in range(4)])
    low = packed[:, : lanes * 16].reshape(4, lanes, 16, 128)
    neighbour_grad = low.transpose(2, 0, 1, 3).reshape(16, 4, width).astype(F32)
    high = packed[:, lanes * 16 :].reshape(4, 2, 32, 128)[:, :, :28]
    kv_grad = high.transpose(2, 1, 0, 3).reshape(28, 2, 4 * HD).astype(F32)
    return kv_grad, neighbour_grad


def solution(mesh):
    five = jax.sharding.Mesh(mesh.devices.reshape(4, 4, 2, 4, 2), AXES)
    dp, mp = ("y", "core"), ("x", "zhi")
    in_specs = (
        P(None, dp, None),
        P(),
        P(None, mp),
        P(mp, None),
        P(None, dp, mp),
        P(None, dp, mp),
        P(None, mp),
        P(None, None, mp),
        P(),
        P(),
    )
    out_specs = (P(("grp", "y", "core"), None, mp), P(mp, dp, None))
    return jax.shard_map(local, mesh=five, in_specs=in_specs, out_specs=out_specs, check_vma=False)
```
